256 devices in a mesh: ctx: 16 (over z, core), head: 16 (over x, y).
Axes of the slice: x: 4, y: 4, z: 8, core: 2. Of those that a mesh axis runs over, the one named last changes fastest.
Arguments:
- x_in: bfloat16 [32768, 8192], P(('ctx', 'head')), may hold values from -6 to 6
- b_in: bfloat16 [32768, 8, 128], P(('ctx', 'head')), may hold values from -5 to 5
- c_in: bfloat16 [32768, 8, 128], P(('ctx', 'head')), may hold values from -0.5 to 0.5
- dt_raw: bfloat16 [32768, 128], P(('ctx', 'head')), may hold values from -2 to 335
- decay_rate: float32 [128], replicated, may hold values from 0 to 1
- dt_bias: float32 [128], replicated, may hold values from -6 to -2
- skip_gain: float32 [128], replicated, may hold values from 0.5 to 1.5
Outputs:
- y_out: bfloat16 [32768, 8192], P(('ctx', 'head'))
The draws below stay inside these ranges and needn't reach their ends.
All inputs are finite; a program needn't handle non-finite values.
Results may differ from the reference program's by a relative error of at most 0.012.
Values may be sent and summed in bfloat16 or wider, within the bound.
A program may use at most 128 MiB of HBM per device.

```python
import math
import jax
import jax.numpy as jnp
from jax import lax

H = 128
P_SIZE = 64
N = 128
G = 8
STRETCH = 256
CTX_LEN = 2048
SEQUENCE_TOKENS = 32768


pulse_count = 2


def head_law(key, slow_share):
    head_order = jax.random.permutation(jax.random.fold_in(key, 11), H)
    slow = head_order < int(slow_share * H)
    factor = jnp.exp(jax.random.uniform(jax.random.fold_in(key, 12), (H,), jnp.float32, math.log(0.25), 0.0))
    jitter = jnp.exp(jax.random.uniform(jax.random.fold_in(key, 13), (H,), jnp.float32, -0.3, 0.3))
    dt_nominal = jnp.where(slow, 0.004, 0.05) * jitter
    rate = jnp.where(slow, factor / (SEQUENCE_TOKENS * 0.004), factor)
    bias_term = dt_nominal + jnp.log(-jnp.expm1(-dt_nominal))
    return (rate, bias_term)


def pulse_rows(key):
    position_list = jax.random.randint(jax.random.fold_in(key, 21), (pulse_count,), 0, SEQUENCE_TOKENS)
    return jnp.zeros((SEQUENCE_TOKENS,), jnp.float32).at[position_list].set(1.0)


def draw_decay_rate(key, part):
    share = 0.5
    rate, bias_term = head_law(key, share)
    return rate


def draw_dt_bias(key, part):
    share = 0.5
    rate, bias_term = head_law(key, share)
    return bias_term


def draw_dt_raw(key, part):
    share = 0.5
    rate, bias_term = head_law(key, share)
    marker_list = pulse_rows(key)
    key = jax.random.fold_in(key, 3)
    coarse_estimate = 0.35 * jnp.clip(jax.random.normal(jax.random.fold_in(key, 1), (SEQUENCE_TOKENS, H), jnp.float32), -4.0, 4.0)
    start_shift = jax.random.uniform(jax.random.fold_in(key, 2), (SEQUENCE_TOKENS // CTX_LEN, 1), jnp.float32, -0.35, 0.35)
    start_shift = jnp.repeat(start_shift, CTX_LEN, axis=0)
    loss = jax.random.uniform(jax.random.fold_in(key, 4), (SEQUENCE_TOKENS, 1), jnp.float32, 0.2, 0.4)
    goal_value = -jnp.log(1.0 - loss) / rate[None, :]
    pulse_value = goal_value + jnp.log(-jnp.expm1(-goal_value)) - bias_term[None, :]
    return jnp.where(marker_list[:, None] > 0.5, pulse_value, coarse_estimate + start_shift).astype(jnp.bfloat16)


def draw_b_in(key, part):
    marker_list = pulse_rows(key)
    key = jax.random.fold_in(key, 5)
    base = jnp.clip(jax.random.normal(key, (SEQUENCE_TOKENS, G, N), jnp.float32), -5.0, 5.0)
    return (base * (1.0 - 0.998 * marker_list[:, None, None])).astype(jnp.bfloat16)


def steps_of(stream_key, shape, split, least, high):
    level, own = 1.0, jax.random.fold_in(stream_key, 6)
    for dim, shards_of in split:
        draws = jnp.exp(jax.random.uniform(jax.random.fold_in(own, dim), (shards_of,), jnp.float32, least / len(split), high / len(split)))
        level = level * jnp.repeat(draws, shape[dim] // shards_of).reshape([-1 if axis == dim else 1 for axis in range(len(shape))])
    return level


def noise(own_key, shape, scale, bound, shards=(), kind=jnp.bfloat16):
    entries = scale * jax.random.normal(own_key, shape, jnp.float32)
    if shards:
        entries = entries * steps_of(own_key, shape, shards, -0.22, 0.18)
    return jnp.clip(entries, -bound, bound).astype(kind)


def setup_inputs(seed: int = 0) -> dict:
    key_of = jax.random.split(jax.random.key(seed), 8)
    x_in = noise(key_of[0], (SEQUENCE_TOKENS, H * P_SIZE), 1.0, 6.0, ((0, 256),))
    b_in = draw_b_in(jax.random.fold_in(key_of[7], 71), 0)
    c_in = noise(key_of[2], (SEQUENCE_TOKENS, G, N), N ** -0.5, 0.5, ((0, 256),))
    dt_raw = draw_dt_raw(jax.random.fold_in(key_of[7], 71), 0)
    decay_rate = draw_decay_rate(jax.random.fold_in(key_of[7], 71), 0)
    dt_bias = draw_dt_bias(jax.random.fold_in(key_of[7], 71), 0)
    skip_gain = jnp.clip(jax.random.uniform(key_of[6], (H,), jnp.float32, 0.5, 1.5), 0.5, 1.5)
    return {"x_in": x_in, "b_in": b_in, "c_in": c_in, "dt_raw": dt_raw, "decay_rate": decay_rate, "dt_bias": dt_bias, "skip_gain": skip_gain}


def block_step(state_now, inputs):
    x_block, b_block, c_block, dt_block, cum_block = inputs
    positions = jnp.arange(STRETCH)
    causal = (positions[:, None] >= positions[None, :])[:, :, None]
    scores = jnp.dot(c_block, b_block.T, preferred_element_type=jnp.float32)
    spans = cum_block[:, None, :] - cum_block[None, :, :]
    decays = jnp.where(causal, jnp.exp(jnp.where(causal, spans, 0.0)), 0.0)
    weights = (scores[:, :, None] * decays * dt_block[None, :, :]).astype(jnp.bfloat16)
    y_inside = jnp.einsum("ijh,jhp->ihp", weights, x_block, preferred_element_type=jnp.float32)
    y_state = jnp.exp(cum_block)[:, :, None] * jnp.einsum("in,hpn->ihp", c_block.astype(jnp.float32), state_now, precision=lax.Precision.HIGHEST)
    end_weight = jnp.exp(cum_block[-1][None, :] - cum_block) * dt_block
    b_scaled = (b_block.astype(jnp.float32)[:, None, :] * end_weight[:, :, None]).astype(jnp.bfloat16)
    state_add = jnp.einsum("jhn,jhp->hpn", b_scaled, x_block, preferred_element_type=jnp.float32)
    state_next = jnp.exp(cum_block[-1])[:, None, None] * state_now + state_add
    return state_next, y_inside + y_state


def group_scan(inputs):
    x_groups = inputs[0]
    state_start = jnp.zeros((x_groups.shape[2], x_groups.shape[3], inputs[1].shape[2]), jnp.float32)
    final_state, outputs = lax.scan(block_step, state_start, inputs)
    return outputs, final_state


def block_scan(x_local, b_local, c_local, dt_local, rate_local, bias_local):
    row_count = x_local.shape[0]
    head_count = dt_local.shape[1]
    groups = b_local.shape[1]
    state_size = b_local.shape[2]
    head_width = x_local.shape[1] // head_count
    per_group = head_count // groups
    blocks = row_count // STRETCH
    step_dt = jax.nn.softplus(dt_local.astype(jnp.float32) + bias_local[None, :])
    log_decay = -rate_local[None, :] * step_dt
    within = jnp.cumsum(log_decay.reshape(blocks, STRETCH, head_count), axis=1)
    totals = within[:, -1, :]
    before = jnp.cumsum(totals, axis=0) - totals
    running = (within + before[:, None, :]).reshape(row_count, head_count)
    x_groups = x_local.reshape(blocks, STRETCH, groups, per_group, head_width).transpose(2, 0, 1, 3, 4)
    b_groups = b_local.reshape(blocks, STRETCH, groups, state_size).transpose(2, 0, 1, 3)
    c_groups = c_local.reshape(blocks, STRETCH, groups, state_size).transpose(2, 0, 1, 3)
    dt_groups = step_dt.reshape(blocks, STRETCH, groups, per_group).transpose(2, 0, 1, 3)
    cum_groups = within.reshape(blocks, STRETCH, groups, per_group).transpose(2, 0, 1, 3)
    outputs, finals = lax.map(group_scan, (x_groups, b_groups, c_groups, dt_groups, cum_groups))
    partial_value = outputs.transpose(1, 2, 0, 3, 4).reshape(row_count, head_count, head_width)
    return partial_value, running, finals.reshape(head_count, head_width, state_size), jnp.sum(log_decay, axis=0)


def reference(x_in, b_in, c_in, dt_raw, decay_rate, dt_bias, skip_gain):
    partial_value, running, finals, shard_log = block_scan(x_in, b_in, c_in, dt_raw, decay_rate, dt_bias)
    direct = skip_gain[None, :, None] * x_in.reshape(SEQUENCE_TOKENS, H, P_SIZE).astype(jnp.float32)
    return (partial_value + direct).astype(jnp.bfloat16).reshape(SEQUENCE_TOKENS, H * P_SIZE)
```

```python
import functools

import jax
import jax.numpy as jnp
from jax import lax
from jax.experimental import pallas as pl
from jax.experimental.pallas import tpu as pltpu
from jax.sharding import PartitionSpec as P

MESH = pl.DeviceIdType.MESH
BF, F32 = jnp.bfloat16, jnp.float32
LOG2E = 1.4426950408889634
ROWS = 128
HEADS, GROUPS, STATE, WIDTH = 128, 8, 128, 64
PER = HEADS // GROUPS
GCOLS = PER * WIDTH
SHARDS = 16
OWN = HEADS // SHARDS * WIDTH
PIECES = 2
COLS = OWN // PIECES
HALF = COLS // 2
XS, YS, ZS = 4, 4, 8
HI = lax.Precision.HIGHEST


def dot(a, b, dims=((1,), (0,)), precision=None):
    return lax.dot_general(a, b, (dims, ((), ())), precision=precision, preferred_element_type=F32)


def two_parts(a):
    hi = a.astype(BF)
    lo = (a - hi.astype(F32)).astype(BF)
    return jnp.concatenate([hi, lo], axis=1)


def iota(shape, dim):
    return lax.broadcasted_iota(jnp.int32, shape, dim)


def kernel(
    x_hbm, b_hbm, c_hbm, dt_ref, rate_ref, bias_ref, skip_ref, y_hbm,
    xv, bv, cv, bg, cg, spread, end_parts, in_parts, skip_parts, cum_cols, cum_rows, dt_rows,
    s_out, s_in, p_out, p_in, acc, ew, yv,
    log_own, log_all, shard_own, shard_all, pair_out, pair_in, zsum_own, zsum_in, back_out, back_in,
    load_sem, b_sem, y_sem, s_send, s_recv, p_send, p_recv, log_send, log_recv,
    shard_send, shard_recv, core_send, core_recv, z_send, z_recv, back_send, back_recv,
):
    ctx, me = lax.axis_index("ctx"), lax.axis_index("head")
    z, core = ctx // 2, lax.rem(ctx, 2)
    mx, my = me // YS, lax.rem(me, YS)
    other = z * 2 + 1 - core

    def peer(i, sign):
        o = lax.rem(i * 7, SHARDS)
        px = lax.rem(mx + XS + sign * (o // YS), XS)
        py = lax.rem(my + YS + sign * lax.rem(o, YS), YS)
        return px * YS + py

    def remote(src, dst, send, recv, c, h):
        return pltpu.make_async_remote_copy(
            src_ref=src, dst_ref=dst, send_sem=send, recv_sem=recv, device_id=(c, h), device_id_type=MESH
        )

    def log_copy(to, slot):
        return remote(log_own, log_all.at[slot], log_send.at[to], log_recv.at[slot], ctx, to)

    def s_copy(p, to, slot):
        return remote(s_out.at[p, to], s_in.at[p, slot], s_send.at[p, to], s_recv.at[p, slot], ctx, to)

    def p_copy(p, to, slot):
        return remote(p_out.at[p, to], p_in.at[p, slot], p_send.at[p, to], p_recv.at[p, slot], ctx, to)

    def shard_core_copy():
        return remote(shard_own.at[core], shard_own.at[core], shard_send.at[ZS], shard_recv.at[ZS], other, me)

    def shard_core_wait():
        return remote(shard_own.at[1 - core], shard_own.at[1 - core], shard_send.at[ZS], shard_recv.at[ZS], other, me)

    def shard_copy(to, slot):
        return remote(shard_own, shard_all.at[slot], shard_send.at[to], shard_recv.at[slot], to * 2 + core, me)

    def z_copy(p, to, slot):
        return remote(zsum_own.at[p], zsum_in.at[p, slot], z_send.at[p, to], z_recv.at[p, slot], to * 2 + core, me)

    def pair_copy(p):
        return remote(pair_out.at[p], pair_in.at[p], core_send.at[p], core_recv.at[p], other, me)

    def back_copy(p):
        return remote(back_out.at[p], back_in.at[p], back_send.at[p], back_recv.at[p], other, me)

    def x_load(g):
        cols = pl.ds(pl.multiple_of(g * GCOLS, GCOLS), GCOLS)
        return pltpu.make_async_copy(x_hbm.at[:, cols], xv.at[:, cols], load_sem.at[g])

    b_load = pltpu.make_async_copy(b_hbm, bv, b_sem.at[0])
    c_load = pltpu.make_async_copy(c_hbm, cv, b_sem.at[1])
    b_load.start()
    for g in range(GROUPS):
        x_load(g).start()
    c_load.start()

    barrier = pltpu.get_barrier_semaphore()

    def greet_head(i, carry):
        pl.semaphore_signal(barrier, inc=1, device_id=(ctx, peer(i, 1)), device_id_type=MESH)
        return carry

    lax.fori_loop(1, SHARDS, greet_head, 0)

    def greet_z(d, carry):
        pl.semaphore_signal(
            barrier, inc=1, device_id=(lax.rem(z + d, ZS) * 2 + core, me), device_id_type=MESH
        )
        return carry

    lax.fori_loop(1, ZS, greet_z, 0)
    pl.semaphore_signal(barrier, inc=1, device_id=(other, me), device_id_type=MESH)

    raw = dt_ref[...].astype(F32) + bias_ref[...]
    step = jnp.maximum(raw, 0.0) + jnp.log1p(jnp.exp(-jnp.abs(raw)))
    log_decay = -rate_ref[...] * step
    lower = iota((ROWS, ROWS), 0) >= iota((ROWS, ROWS), 1)
    within = dot(lower.astype(F32), log_decay, precision=HI)
    total = within[ROWS - 1 : ROWS, :]
    log_own[...] = jnp.broadcast_to(total, (8, HEADS))
    end_weight = two_parts(jnp.exp(total - within) * step)
    in_weight = two_parts(jnp.exp(within))
    skip_hl = two_parts(jnp.broadcast_to(skip_ref[...], (16, HEADS)))
    scaled = within * LOG2E
    scaled_t = jnp.transpose(scaled)
    step_t = jnp.transpose(step)
    for g in range(GROUPS):
        lo, hi = g * PER, (g + 1) * PER
        for ref, value in ((end_parts, end_weight), (in_parts, in_weight), (skip_parts, skip_hl)):
            ref[g] = jnp.concatenate([value[:, lo:hi], value[:, HEADS + lo : HEADS + hi]], axis=1)
        cum_cols[g] = scaled[:, lo:hi]
        cum_rows[g] = scaled_t[lo:hi, :]
        dt_rows[g] = step_t[lo:hi, :]
    spread[...] = (lax.rem(iota((2 * PER, GCOLS), 0), PER) == iota((2 * PER, GCOLS), 1) // WIDTH).astype(BF)

    order_row, order_col = iota((256, 256), 0), iota((256, 256), 1)
    order = (order_col == lax.rem(order_row, 32) * GROUPS + order_row // 32).astype(BF)

    def regroup(src, dst):
        for strip in range(ROWS // 32):
            part = dot(order, src[strip * 256 : (strip + 1) * 256, :]).astype(BF)
            for g in range(GROUPS):
                dst[g, strip * 32 : (strip + 1) * 32, :] = part[g * 32 : (g + 1) * 32, :]

    b_load.wait()
    regroup(bv, bg)

    def own_state(g, carry):
        x_load(g).wait()
        cols = pl.ds(pl.multiple_of(g * GCOLS, GCOLS), GCOLS)
        weight = dot(end_parts[g], spread[...])
        xs = (xv[:, cols].astype(F32) * weight).astype(BF)
        value = dot(bg[g], xs, ((0,), (0,))).astype(BF)
        for a in range(2):
            for p in range(PIECES):
                at = a * OWN + p * COLS
                s_out[p, 2 * g + a] = value[:, at : at + COLS]
        return carry

    lax.fori_loop(0, GROUPS, own_state, 0)

    pl.semaphore_wait(barrier, SHARDS - 1 + ZS - 1 + 1)

    def send_logs(i, carry):
        log_copy(peer(i, 1), me).start()
        return carry

    lax.fori_loop(1, SHARDS, send_logs, 0)
    for p in range(PIECES):

        def send_s(i, carry):
            s_copy(p, peer(i, 1), me).start()
            return carry

        lax.fori_loop(1, SHARDS, send_s, 0)

    c_load.wait()
    regroup(cv, cg)

    lane = iota((ROWS, 2 * WIDTH), 1)

    def inside(g, carry):
        scores = jnp.where(lower, dot(cg[g], bg[g], ((1,), (1,))), 0.0)
        skip = dot(skip_parts[g], spread[...])
        col, row, dts = cum_cols[g], cum_rows[g], dt_rows[g]
        for pair in range(PER // 2):
            parts = []
            for h in (2 * pair, 2 * pair + 1):
                span = col[:, h : h + 1] - row[h : h + 1, :]
                decay = jnp.exp2(jnp.minimum(span, 0.0))
                parts.append((scores * decay * dts[h : h + 1, :]).astype(BF))
            at = pair * 2 * WIDTH
            x2 = xv[:, pl.ds(pl.multiple_of(g * GCOLS + at, 2 * WIDTH), 2 * WIDTH)]
            zero = jnp.zeros_like(x2)
            blocks = jnp.concatenate(
                [jnp.where(lane < WIDTH, x2, zero), jnp.where(lane < WIDTH, zero, x2)], axis=0
            )
            value = dot(jnp.concatenate(parts, axis=1), blocks)
            value = value + skip[0:1, at : at + 2 * WIDTH] * x2.astype(F32)
            acc[2 * g + at // OWN, :, at % OWN : at % OWN + 2 * WIDTH] = value
        weight = dot(in_parts[g], spread[...])
        ew[2 * g] = weight[:, :OWN]
        ew[2 * g + 1] = weight[:, OWN:]
        return carry

    lax.fori_loop(0, 3, inside, 0)

    def logs_in(i, carry):
        src = peer(i, -1)
        log_copy(src, src).wait_recv()
        return carry

    lax.fori_loop(1, SHARDS, logs_in, 0)
    log_all[me] = log_own[...]
    logs = log_all[:, 0, :]
    shard_log = jnp.sum(logs, axis=0, keepdims=True)
    shard_own[core] = jnp.broadcast_to(shard_log, (8, HEADS))
    shard_core_copy().start()
    later = (iota((SHARDS, SHARDS), 1) > iota((SHARDS, SHARDS), 0)).astype(F32)
    to_end = dot(later, logs, precision=HI)
    mine = (iota((HEADS, OWN), 0) == me * (HEADS // SHARDS) + iota((HEADS, OWN), 1) // WIDTH).astype(F32)
    chunk_decay = jnp.exp(dot(logs, mine, precision=HI))
    end_decay = jnp.exp(dot(to_end, mine, precision=HI))

    lax.fori_loop(3, 4, inside, 0)
    shard_core_wait().wait_recv()

    def send_shard(d, carry):
        shard_copy(lax.rem(z + d, ZS), z).start()
        return carry

    lax.fori_loop(1, ZS, send_shard, 0)
    lax.fori_loop(4, GROUPS, inside, 0)

    def shard_wait(d, carry):
        src = lax.rem(z + ZS - d, ZS)
        shard_copy(src, src).wait_recv()
        return carry

    lax.fori_loop(1, ZS, shard_wait, 0)
    shard_all[z] = shard_own[...]
    shard_logs = shard_all[:, :, 0, :]
    pair_logs = shard_logs[:, 0, :] + shard_logs[:, 1, :]
    zi, zj = iota((ZS, ZS), 0), iota((ZS, ZS), 1)
    between = ((zj > zi) & (zj < z)).astype(F32)
    z_logs = dot(between, pair_logs, precision=HI)
    z_weight = jnp.where(iota((ZS, OWN), 0) < z, jnp.exp(dot(z_logs, mine, precision=HI)), 0.0)
    pair_decay = jnp.exp(dot(shard_all[z, :, 0, :], mine, precision=HI))

    def mine_half(value):
        return jnp.where(core == 0, value[:, :HALF], value[:, HALF:])

    def gather(p):
        cols = slice(p * COLS, (p + 1) * COLS)

        def s_wait(i, carry):
            src = peer(i, -1)
            s_copy(p, src, src).wait_recv()
            return carry

        lax.fori_loop(1, SHARDS, s_wait, 0)
        s_in[p, me] = s_out[p, me]
        value = s_in[p, SHARDS - 1].astype(F32)
        for j in range(SHARDS - 1):
            value += end_decay[j : j + 1, cols] * s_in[p, j].astype(F32)
        keep = mine_half(value)
        pair_out[p] = jnp.where(core == 0, value[:, HALF:], value[:, :HALF]).astype(BF)
        pair_copy(p).start()
        pair_copy(p).wait_recv()
        theirs = pair_in[p].astype(F32)
        first = jnp.where(core == 0, keep, theirs)
        second = jnp.where(core == 0, theirs, keep)
        decay = mine_half(pair_decay[1:2, cols])
        zsum_own[p] = (first * decay + second).astype(BF)

        def z_start(d, carry):
            z_copy(p, lax.rem(z + d, ZS), z).start()
            return carry

        lax.fori_loop(1, ZS, z_start, 0)
        return first

    def give_back(p, first):
        cols = slice(p * COLS, (p + 1) * COLS)

        def z_wait(d, carry):
            src = lax.rem(z + ZS - d, ZS)
            z_copy(p, src, src).wait_recv()
            return carry

        lax.fori_loop(1, ZS, z_wait, 0)
        zsum_in[p, z] = zsum_own[p]
        weight = mine_half(z_weight[:, cols])
        before = jnp.zeros((STATE, HALF), F32)
        for j in range(ZS - 1):
            before += weight[j : j + 1, :] * zsum_in[p, j].astype(F32)
        after = before * mine_half(pair_decay[0:1, cols]) + first
        back_out[p] = jnp.where(core == 0, after, before).astype(BF)
        back_copy(p).start()
        back_copy(p).wait_recv()
        keep = jnp.where(core == 0, before, after)
        theirs = back_in[p].astype(F32)
        state = jnp.where(
            core == 0, jnp.concatenate([keep, theirs], axis=1), jnp.concatenate([theirs, keep], axis=1)
        )
        for j in range(SHARDS):
            p_out[p, j] = state.astype(BF)
            if j < SHARDS - 1:
                state = state * chunk_decay[j : j + 1, cols] + s_in[p, j].astype(F32)
        p_in[p, me] = p_out[p, me]

        def p_start(i, carry):
            p_copy(p, peer(i, 1), me).start()
            return carry

        lax.fori_loop(1, SHARDS, p_start, 0)

    def y_store(k):
        cols = pl.ds(pl.multiple_of(k * OWN, OWN), OWN)
        return pltpu.make_async_copy(yv.at[k], y_hbm.at[:, cols], y_sem.at[k])

    def finish(p, k):
        across = dot(cg[k // 2], p_in[p, k])
        cols = slice(p * COLS, (p + 1) * COLS)
        yv[k, :, cols] = (acc[k, :, cols] + ew[k, :, cols] * across).astype(BF)
        if p == PIECES - 1:
            y_store(k).start()

    firsts = {}
    firsts[0] = gather(0)
    give_back(0, firsts[0])
    firsts[1] = gather(1)
    give_back(1, firsts[1])
    for p in range(PIECES):
        finish(p, me)

        def p_wait(i, carry):
            src = peer(i, -1)
            p_copy(p, src, src).wait_recv()
            finish(p, src)
            return carry

        lax.fori_loop(1, SHARDS, p_wait, 0)

    def sent_head(i, carry):
        to = peer(i, 1)
        log_copy(to, me).wait_send()
        for p in range(PIECES):
            s_copy(p, to, me).wait_send()
            p_copy(p, to, me).wait_send()
        return carry

    lax.fori_loop(1, SHARDS, sent_head, 0)

    def sent_z(d, carry):
        to = lax.rem(z + d, ZS)
        shard_copy(to, z).wait_send()
        for p in range(PIECES):
            z_copy(p, to, z).wait_send()
        return carry

    lax.fori_loop(1, ZS, sent_z, 0)
    shard_core_copy().wait_send()
    for p in range(PIECES):
        pair_copy(p).wait_send()
        back_copy(p).wait_send()

    def stored(k, carry):
        y_store(k).wait()
        return carry

    lax.fori_loop(0, SHARDS, stored, 0)


def per_device(x_in, b_in, c_in, dt_raw, decay_rate, dt_bias, skip_gain):
    vmem, dma = pltpu.VMEM, pltpu.SemaphoreType.DMA
    any_spec, vmem_spec = pl.BlockSpec(memory_space=pl.ANY), pl.BlockSpec(memory_space=pltpu.VMEM)
    return pl.pallas_call(
        kernel,
        name="scan",
        out_shape=jax.ShapeDtypeStruct((ROWS, HEADS * WIDTH), BF),
        in_specs=[any_spec] * 3 + [vmem_spec] * 4,
        out_specs=any_spec,
        scratch_shapes=[
            vmem((ROWS, HEADS * WIDTH), BF),
            vmem((ROWS * GROUPS, STATE), BF),
            vmem((ROWS * GROUPS, STATE), BF),
            vmem((GROUPS, ROWS, STATE), BF),
            vmem((GROUPS, ROWS, STATE), BF),
            vmem((2 * PER, GCOLS), BF),
            vmem((GROUPS, ROWS, 2 * PER), BF),
            vmem((GROUPS, ROWS, 2 * PER), BF),
            vmem((GROUPS, 16, 2 * PER), BF),
            vmem((GROUPS, ROWS, PER), F32),
            vmem((GROUPS, PER, ROWS), F32),
            vmem((GROUPS, PER, ROWS), F32),
            vmem((PIECES, SHARDS, STATE, COLS), BF),
            vmem((PIECES, SHARDS, STATE, COLS), BF),
            vmem((PIECES, SHARDS, STATE, COLS), BF),
            vmem((PIECES, SHARDS, STATE, COLS), BF),
            vmem((SHARDS, ROWS, OWN), F32),
            vmem((SHARDS, ROWS, OWN), F32),
            vmem((SHARDS, ROWS, OWN), BF),
            vmem((8, HEADS), F32),
            vmem((SHARDS, 8, HEADS), F32),
            vmem((2, 8, HEADS), F32),
            vmem((ZS, 2, 8, HEADS), F32),
            vmem((PIECES, STATE, HALF), BF),
            vmem((PIECES, STATE, HALF), BF),
            vmem((PIECES, STATE, HALF), BF),
            vmem((PIECES, ZS, STATE, HALF), BF),
            vmem((PIECES, STATE, HALF), BF),
            vmem((PIECES, STATE, HALF), BF),
            dma((GROUPS,)),
            dma((2,)),
            dma((SHARDS,)),
            dma((PIECES, SHARDS)),
            dma((PIECES, SHARDS)),
            dma((PIECES, SHARDS)),
            dma((PIECES, SHARDS)),
            dma((SHARDS,)),
            dma((SHARDS,)),
            dma((ZS + 1,)),
            dma((ZS + 1,)),
            dma((PIECES,)),
            dma((PIECES,)),
            dma((PIECES, ZS)),
            dma((PIECES, ZS)),
            dma((PIECES,)),
            dma((PIECES,)),
        ],
        compiler_params=pltpu.CompilerParams(
            collective_id=0, has_side_effects=True, vmem_limit_bytes=48 * 1024 * 1024
        ),
    )(
        x_in,
        b_in.reshape(ROWS * GROUPS, STATE),
        c_in.reshape(ROWS * GROUPS, STATE),
        dt_raw,
        decay_rate.reshape(1, HEADS),
        dt_bias.reshape(1, HEADS),
        skip_gain.reshape(1, HEADS),
    )


def solution(mesh):
    rows = ("ctx", "head")
    in_specs = (P(rows, None), P(rows, None, None), P(rows, None, None), P(rows, None), P(), P(), P())
    return jax.shard_map(
        per_device, mesh=mesh, in_specs=in_specs, out_specs=P(rows, None), check_vma=False
    )
```

```python
import functools

import jax
import jax.numpy as jnp
from jax import lax
from jax.experimental import pallas as pl
from jax.experimental.pallas import tpu as pltpu
from jax.sharding import PartitionSpec as P

MESH = pl.DeviceIdType.MESH
BF, F32 = jnp.bfloat16, jnp.float32
LOG2E = 1.4426950408889634
ROWS = 128
HEADS, GROUPS, STATE, WIDTH = 128, 8, 128, 64
PER = HEADS // GROUPS
GCOLS = PER * WIDTH
SHARDS = 16
OWN = HEADS // SHARDS * WIDTH
PIECES = 4
COLS = OWN // PIECES
HALF = STATE // 2
XS, YS, ZS = 4, 4, 8
HI = lax.Precision.HIGHEST


def dot(a, b, dims=((1,), (0,)), precision=None):
    return lax.dot_general(a, b, (dims, ((), ())), precision=precision, preferred_element_type=F32)


def two_parts(a):
    hi = a.astype(BF)
    lo = (a - hi.astype(F32)).astype(BF)
    return jnp.concatenate([hi, lo], axis=1)


def iota(shape, dim):
    return lax.broadcasted_iota(jnp.int32, shape, dim)


def kernel(
    x_hbm, b_hbm, c_hbm, dt_hbm, rate_hbm, bias_hbm, skip_hbm, y_ref,
    dt_ref, rate_ref, bias_ref, skip_ref, xv, bv, cv, bg, cg, spread, end_parts, in_parts, skip_parts, cum_cols, cum_rows, dt_rows,
    s_out, s_in, p_out, p_in, acc, ew,
    log_own, log_all, shard_own, shard_all, pair_out, pair_in, zsum_own, zsum_in, back_out, back_in,
    end_rows, z_rows, total_state, before_state, firsts,
    load_sem, b_sem, s_send, s_recv, p_send, p_recv, log_send, log_recv,
    shard_send, shard_recv, core_send, core_recv, z_send, z_recv, back_send, back_recv,
):
    ctx, me = lax.axis_index("ctx"), lax.axis_index("head")
    z, core = ctx // 2, lax.rem(ctx, 2)
    mx, my = me // YS, lax.rem(me, YS)
    other = z * 2 + 1 - core

    def peer(i, sign):
        o = lax.rem(i * 7, SHARDS)
        px = lax.rem(mx + XS + sign * (o // YS), XS)
        py = lax.rem(my + YS + sign * lax.rem(o, YS), YS)
        return px * YS + py

    def remote(src, dst, send, recv, c, h):
        return pltpu.make_async_remote_copy(
            src_ref=src, dst_ref=dst, send_sem=send, recv_sem=recv, device_id=(c, h), device_id_type=MESH
        )

    def log_copy(to, slot):
        return remote(log_own, log_all.at[slot], log_send.at[to], log_recv.at[slot], ctx, to)

    def s_copy(p, to, slot):
        return remote(s_out.at[p, to], s_in.at[p, slot], s_send.at[p, to], s_recv.at[p, slot], ctx, to)

    def p_copy(p, to, slot):
        return remote(p_out.at[p, to], p_in.at[p, slot], p_send.at[p, to], p_recv.at[p, slot], ctx, to)

    def shard_core_copy():
        return remote(shard_own.at[core], shard_own.at[core], shard_send.at[ZS], shard_recv.at[ZS], other, me)

    def shard_core_wait():
        return remote(shard_own.at[1 - core], shard_own.at[1 - core], shard_send.at[ZS], shard_recv.at[ZS], other, me)

    def shard_copy(to, slot):
        return remote(shard_own, shard_all.at[slot], shard_send.at[to], shard_recv.at[slot], to * 2 + core, me)

    def z_copy(p, to, slot):
        return remote(zsum_own.at[p], zsum_in.at[p, slot], z_send.at[p, to], z_recv.at[p, slot], to * 2 + core, me)

    def pair_copy(p):
        return remote(pair_out.at[p], pair_in.at[p], core_send.at[p], core_recv.at[p], other, me)

    def back_copy(p):
        return remote(back_out.at[p], back_in.at[p], back_send.at[p], back_recv.at[p], other, me)

    def x_load(g):
        cols = pl.ds(pl.multiple_of(g * GCOLS, GCOLS), GCOLS)
        return pltpu.make_async_copy(x_hbm.at[:, cols], xv.at[:, cols], load_sem.at[g])

    b_load = pltpu.make_async_copy(b_hbm, bv, b_sem.at[0])
    c_load = pltpu.make_async_copy(c_hbm, cv, b_sem.at[1])
    small = [
        pltpu.make_async_copy(src, dst, b_sem.at[2 + i])
        for i, (src, dst) in enumerate(
            ((dt_hbm, dt_ref), (rate_hbm, rate_ref), (bias_hbm, bias_ref), (skip_hbm, skip_ref))
        )
    ]
    for load in small:
        load.start()
    b_load.start()

    def start_load(i, carry):
        x_load(lax.rem(me // 2 + 1 + i, GROUPS)).start()
        return carry

    lax.fori_loop(0, GROUPS, start_load, 0)
    c_load.start()

    shard_all[...] = jnp.zeros_like(shard_all)
    barrier = pltpu.get_barrier_semaphore()

    def greet_head(i, carry):
        pl.semaphore_signal(barrier, inc=1, device_id=(ctx, peer(i, 1)), device_id_type=MESH)
        return carry

    lax.fori_loop(1, SHARDS, greet_head, 0)

    def greet_z(back, carry):
        pl.semaphore_signal(barrier, inc=1, device_id=(back * 2 + core, me), device_id_type=MESH)
        return carry

    lax.fori_loop(0, z, greet_z, 0)
    pl.semaphore_signal(barrier, inc=1, device_id=(other, me), device_id_type=MESH)

    for load in small:
        load.wait()
    raw = dt_ref[...].astype(F32) + bias_ref[...]
    step = jnp.maximum(raw, 0.0) + jnp.log1p(jnp.exp(-jnp.abs(raw)))
    log_decay = -rate_ref[...] * step
    lower = iota((ROWS, ROWS), 0) >= iota((ROWS, ROWS), 1)
    within = dot(lower.astype(F32), log_decay, precision=HI)
    total = within[ROWS - 1 : ROWS, :]
    log_own[...] = jnp.broadcast_to(total, (8, HEADS))
    end_weight = two_parts(jnp.exp(total - within) * step)
    in_weight = two_parts(jnp.exp(within))
    skip_hl = two_parts(jnp.broadcast_to(skip_ref[...], (16, HEADS)))
    scaled = within * LOG2E
    scaled_t = jnp.transpose(scaled)
    step_t = jnp.transpose(step)
    for g in range(GROUPS):
        lo, hi = g * PER, (g + 1) * PER
        for ref, value in ((end_parts, end_weight), (in_parts, in_weight), (skip_parts, skip_hl)):
            ref[g] = jnp.concatenate([value[:, lo:hi], value[:, HEADS + lo : HEADS + hi]], axis=1)
        cum_cols[g] = scaled[:, lo:hi]
        cum_rows[g] = scaled_t[lo:hi, :]
        dt_rows[g] = step_t[lo:hi, :]
    spread[...] = (lax.rem(iota((2 * PER, GCOLS), 0), PER) == iota((2 * PER, GCOLS), 1) // WIDTH).astype(BF)

    order_row, order_col = iota((256, 256), 0), iota((256, 256), 1)
    order = (order_col == lax.rem(order_row, 32) * GROUPS + order_row // 32).astype(BF)

    def regroup(src, dst):
        for strip in range(ROWS // 32):
            part = dot(order, src[strip * 256 : (strip + 1) * 256, :]).astype(BF)
            for g in range(GROUPS):
                dst[g, strip * 32 : (strip + 1) * 32, :] = part[g * 32 : (g + 1) * 32, :]

    b_load.wait()
    regroup(bv, bg)

    pl.semaphore_wait(barrier, SHARDS - 1 + ZS - 1 - z + 1)

    def send_logs(i, carry):
        log_copy(peer(i, 1), me).start()
        return carry

    lax.fori_loop(1, SHARDS, send_logs, 0)

    def own_state(i, carry):
        g = lax.rem(me // 2 + 1 + i, GROUPS)
        x_load(g).wait()
        cols = pl.ds(pl.multiple_of(g * GCOLS, GCOLS), GCOLS)
        weight = dot(end_parts[g], spread[...])
        xs = (xv[:, cols].astype(F32) * weight).astype(BF)
        value = dot(bg[g], xs, ((0,), (0,))).astype(BF)
        for a in range(2):
            for p in range(PIECES):
                at = a * OWN + p * COLS
                s_out[p, 2 * g + a] = value[:, at : at + COLS]
        for a in range(2):

            @pl.when(2 * g + a != me)
            def _():
                s_copy(0, 2 * g + a, me).start()

        return carry

    lax.fori_loop(0, GROUPS, own_state, 0)
    for p in range(1, PIECES):

        def send_s(i, carry):
            s_copy(p, peer(i, 1), me).start()
            return carry

        lax.fori_loop(1, SHARDS, send_s, 0)

    c_load.wait()
    regroup(cv, cg)

    lane = iota((ROWS, 2 * WIDTH), 1)

    def inside(g, carry):
        scores = jnp.where(lower, dot(cg[g], bg[g], ((1,), (1,))), 0.0)
        skip = dot(skip_parts[g], spread[...])
        col, row, dts = cum_cols[g], cum_rows[g], dt_rows[g]
        for pair in range(PER // 2):
            parts = []
            for h in (2 * pair, 2 * pair + 1):
                span = col[:, h : h + 1] - row[h : h + 1, :]
                decay = jnp.exp2(jnp.minimum(span, 0.0))
                parts.append((scores * decay * dts[h : h + 1, :]).astype(BF))
            at = pair * 2 * WIDTH
            x2 = xv[:, pl.ds(pl.multiple_of(g * GCOLS + at, 2 * WIDTH), 2 * WIDTH)]
            zero = jnp.zeros_like(x2)
            blocks = jnp.concatenate(
                [jnp.where(lane < WIDTH, x2, zero), jnp.where(lane < WIDTH, zero, x2)], axis=0
            )
            value = dot(jnp.concatenate(parts, axis=1), blocks)
            value = value + skip[0:1, at : at + 2 * WIDTH] * x2.astype(F32)
            acc[2 * g + at // OWN, :, at % OWN : at % OWN + 2 * WIDTH] = value
        weight = dot(in_parts[g], spread[...])
        ew[2 * g] = weight[:, :OWN]
        ew[2 * g + 1] = weight[:, OWN:]
        return carry

    lax.fori_loop(0, 2, inside, 0)

    def logs_in(i, carry):
        src = peer(i, -1)
        log_copy(src, src).wait_recv()
        return carry

    lax.fori_loop(1, SHARDS, logs_in, 0)
    log_all[me] = log_own[...]
    logs = log_all[:, 0, :]
    shard_log = jnp.sum(logs, axis=0, keepdims=True)
    shard_own[core] = jnp.broadcast_to(shard_log, (8, HEADS))
    shard_core_copy().start()
    later = (iota((SHARDS, SHARDS), 1) > iota((SHARDS, SHARDS), 0)).astype(F32)
    to_end = dot(later, logs, precision=HI)
    mine = (iota((HEADS, OWN), 0) == me * (HEADS // SHARDS) + iota((HEADS, OWN), 1) // WIDTH).astype(F32)
    chunk_decay = jnp.exp(dot(logs, mine, precision=HI))
    end_decay = jnp.exp(dot(to_end, mine, precision=HI))
    for j in range(SHARDS):
        end_rows[j] = jnp.broadcast_to(end_decay[j : j + 1, :], (8, OWN))

    lax.fori_loop(2, 4, inside, 0)
    shard_core_wait().wait_recv()

    def send_shard(to, carry):
        shard_copy(to, z).start()
        return carry

    lax.fori_loop(z + 1, ZS, send_shard, 0)

    def shard_wait(src, carry):
        shard_copy(src, src).wait_recv()
        return carry

    lax.fori_loop(0, z, shard_wait, 0)
    shard_all[z] = shard_own[...]
    shard_logs = shard_all[:, :, 0, :]
    pair_logs = shard_logs[:, 0, :] + shard_logs[:, 1, :]
    zi, zj = iota((ZS, ZS), 0), iota((ZS, ZS), 1)
    between = ((zj > zi) & (zj < z)).astype(F32)
    z_logs = dot(between, pair_logs, precision=HI)
    z_weight = jnp.exp(dot(z_logs, mine, precision=HI))
    for j in range(ZS):
        z_rows[j] = jnp.broadcast_to(z_weight[j : j + 1, :], (8, OWN))
    pair_decay = jnp.exp(dot(shard_all[z, :, 0, :], mine, precision=HI))

    def half(value, which):
        return jnp.where(which == 0, value[:HALF, :], value[HALF:, :])

    def gather(p):
        cols = slice(p * COLS, (p + 1) * COLS)
        s_in[p, me] = s_out[p, me]
        total_state[...] = end_rows[me][0:1, cols] * s_in[p, me].astype(F32)

        def s_wait(i, carry):
            src = peer(i, -1)
            s_copy(p, src, src).wait_recv()
            total_state[...] += end_rows[src][0:1, cols] * s_in[p, src].astype(F32)
            return carry

        lax.fori_loop(1, SHARDS, s_wait, 0)
        value = total_state[...]
        keep = half(value, core)
        pair_out[p] = half(value, 1 - core).astype(BF)
        pair_copy(p).start()
        pair_copy(p).wait_recv()
        theirs = pair_in[p].astype(F32)
        first = jnp.where(core == 0, keep, theirs)
        second = jnp.where(core == 0, theirs, keep)
        zsum_own[p] = (first * pair_decay[1:2, cols] + second).astype(BF)

        def z_start(to, carry):
            z_copy(p, to, z).start()
            return carry

        lax.fori_loop(z + 1, ZS, z_start, 0)
        firsts[p] = first

    def give_back(p):
        cols = slice(p * COLS, (p + 1) * COLS)
        before_state[...] = jnp.zeros_like(before_state)

        def z_wait(src, carry):
            z_copy(p, src, src).wait_recv()
            before_state[...] += z_rows[src][0:1, cols] * zsum_in[p, src].astype(F32)
            return carry

        lax.fori_loop(0, z, z_wait, 0)
        before = before_state[...]
        after = before * pair_decay[0:1, cols] + firsts[p]
        back_out[p] = jnp.where(core == 0, after, before).astype(BF)
        back_copy(p).start()
        back_copy(p).wait_recv()
        keep = jnp.where(core == 0, before, after)
        theirs = back_in[p].astype(F32)
        state = jnp.where(
            core == 0, jnp.concatenate([keep, theirs], axis=0), jnp.concatenate([theirs, keep], axis=0)
        )
        for j in range(SHARDS):
            p_out[p, j] = state.astype(BF)
            if j < SHARDS - 1:
                state = state * chunk_decay[j : j + 1, cols] + s_in[p, j].astype(F32)
        p_in[p, me] = p_out[p, me]

        def p_start(i, carry):
            p_copy(p, peer(i, 1), me).start()
            return carry

        lax.fori_loop(1, SHARDS, p_start, 0)

    def finish(p, k):
        across = dot(cg[k // 2], p_in[p, k])
        cols = slice(p * COLS, (p + 1) * COLS)
        value = (acc[k, :, cols] + ew[k, :, cols] * across).astype(BF)
        y_ref[:, pl.ds(pl.multiple_of(k * OWN + p * COLS, COLS), COLS)] = value

    gather(0)
    lax.fori_loop(4, 6, inside, 0)
    gather(1)
    give_back(0)
    lax.fori_loop(6, 7, inside, 0)
    gather(2)
    give_back(1)
    lax.fori_loop(7, GROUPS, inside, 0)
    gather(3)
    give_back(2)
    give_back(3)
    for p in range(PIECES):
        finish(p, me)

        def p_wait(i, carry):
            batch = [peer(3 * i + 1 + j, -1) for j in range(3)]
            for src in batch:
                p_copy(p, src, src).wait_recv()
            for src in batch:
                finish(p, src)
            return carry

        lax.fori_loop(0, (SHARDS - 1) // 3, p_wait, 0)

    def sent_head(i, carry):
        to = peer(i, 1)
        log_copy(to, me).wait_send()
        for p in range(PIECES):
            s_copy(p, to, me).wait_send()
            p_copy(p, to, me).wait_send()
        return carry

    lax.fori_loop(1, SHARDS, sent_head, 0)

    def sent_z(to, carry):
        shard_copy(to, z).wait_send()
        for p in range(PIECES):
            z_copy(p, to, z).wait_send()
        return carry

    lax.fori_loop(z + 1, ZS, sent_z, 0)
    shard_core_copy().wait_send()
    for p in range(PIECES):
        pair_copy(p).wait_send()
        back_copy(p).wait_send()


def per_device(x_in, b_in, c_in, dt_raw, decay_rate, dt_bias, skip_gain):
    vmem, dma = pltpu.VMEM, pltpu.SemaphoreType.DMA
    any_spec = pl.BlockSpec(memory_space=pltpu.HBM)
    return pl.pallas_call(
        kernel,
        name="scan",
        out_shape=pltpu.VMEM((ROWS, HEADS * WIDTH), BF),
        in_specs=[any_spec] * 7,
        out_specs=pl.BlockSpec(memory_space=pltpu.VMEM),
        scratch_shapes=[
            vmem((ROWS, HEADS), BF),
            vmem((1, HEADS), F32),
            vmem((1, HEADS), F32),
            vmem((1, HEADS), F32),
            vmem((ROWS, HEADS * WIDTH), BF),
            vmem((ROWS * GROUPS, STATE), BF),
            vmem((ROWS * GROUPS, STATE), BF),
            vmem((GROUPS, ROWS, STATE), BF),
            vmem((GROUPS, ROWS, STATE), BF),
            vmem((2 * PER, GCOLS), BF),
            vmem((GROUPS, ROWS, 2 * PER), BF),
            vmem((GROUPS, ROWS, 2 * PER), BF),
            vmem((GROUPS, 16, 2 * PER), BF),
            vmem((GROUPS, ROWS, PER), F32),
            vmem((GROUPS, PER, ROWS), F32),
            vmem((GROUPS, PER, ROWS), F32),
            vmem((PIECES, SHARDS, STATE, COLS), BF),
            vmem((PIECES, SHARDS, STATE, COLS), BF),
            vmem((PIECES, SHARDS, STATE, COLS), BF),
            vmem((PIECES, SHARDS, STATE, COLS), BF),
            vmem((SHARDS, ROWS, OWN), F32),
            vmem((SHARDS, ROWS, OWN), F32),
            vmem((8, HEADS), F32),
            vmem((SHARDS, 8, HEADS), F32),
            vmem((2, 8, HEADS), F32),
            vmem((ZS, 2, 8, HEADS), F32),
            vmem((PIECES, HALF, COLS), BF),
            vmem((PIECES, HALF, COLS), BF),
            vmem((PIECES, HALF, COLS), BF),
            vmem((PIECES, ZS, HALF, COLS), BF),
            vmem((PIECES, HALF, COLS), BF),
            vmem((PIECES, HALF, COLS), BF),
            vmem((SHARDS, 8, OWN), F32),
            vmem((ZS, 8, OWN), F32),
            vmem((STATE, COLS), F32),
            vmem((HALF, COLS), F32),
            vmem((PIECES, HALF, COLS), F32),
            dma((GROUPS,)),
            dma((6,)),
            dma((PIECES, SHARDS)),
            dma((PIECES, SHARDS)),
            dma((PIECES, SHARDS)),
            dma((PIECES, SHARDS)),
            dma((SHARDS,)),
            dma((SHARDS,)),
            dma((ZS + 1,)),
            dma((ZS + 1,)),
            dma((PIECES,)),
            dma((PIECES,)),
            dma((PIECES, ZS)),
            dma((PIECES, ZS)),
            dma((PIECES,)),
            dma((PIECES,)),
        ],
        compiler_params=pltpu.CompilerParams(
            collective_id=0, has_side_effects=True, vmem_limit_bytes=61 * 1024 * 1024
        ),
    )(
        x_in,
        b_in.reshape(ROWS * GROUPS, STATE),
        c_in.reshape(ROWS * GROUPS, STATE),
        dt_raw,
        decay_rate.reshape(1, HEADS),
        dt_bias.reshape(1, HEADS),
        skip_gain.reshape(1, HEADS),
    )


def solution(mesh):
    rows = ("ctx", "head")
    in_specs = (P(rows, None), P(rows, None, None), P(rows, None, None), P(rows, None), P(), P(), P())
    return jax.shard_map(
        per_device, mesh=mesh, in_specs=in_specs, out_specs=P(rows, None), check_vma=False
    )
```

```python
import functools

import jax
import jax.numpy as jnp
from jax import lax
from jax.experimental import pallas as pl
from jax.experimental.pallas import tpu as pltpu
from jax.sharding import PartitionSpec as P

MESH = pl.DeviceIdType.MESH
BF, F32 = jnp.bfloat16, jnp.float32
LOG2E = 1.4426950408889634
ROWS = 128
HEADS, GROUPS, STATE, WIDTH = 128, 8, 128, 64
PER = HEADS // GROUPS
GCOLS = PER * WIDTH
SHARDS = 16
OWN = HEADS // SHARDS * WIDTH
PIECES = 4
COLS = OWN // PIECES
HALF = STATE // 2
XS, YS, ZS = 4, 4, 8
HI = lax.Precision.HIGHEST


def dot(a, b, dims=((1,), (0,)), precision=None):
    return lax.dot_general(a, b, (dims, ((), ())), precision=precision, preferred_element_type=F32)


def two_parts(a):
    hi = a.astype(BF)
    lo = (a - hi.astype(F32)).astype(BF)
    return jnp.concatenate([hi, lo], axis=1)


def iota(shape, dim):
    return lax.broadcasted_iota(jnp.int32, shape, dim)


def kernel(
    x_hbm, b_hbm, c_hbm, dt_hbm, rate_hbm, bias_hbm, skip_hbm, y_ref,
    dt_ref, rate_ref, bias_ref, skip_ref, xv, bv, cv, bg, cg, spread, end_parts, in_parts, skip_parts, cum_cols, cum_rows, dt_rows,
    s_out, s_in, p_out, p_in, acc, ew,
    log_own, log_all, shard_own, shard_all, pair_out, pair_in, zsum_own, zsum_in, back_out, back_in,
    end_rows, z_rows, total_state, before_state, firsts, ready,
    load_sem, b_sem, s_send, s_recv, p_send, p_recv, log_send, log_recv,
    shard_send, shard_recv, core_send, core_recv, z_send, z_recv, back_send, back_recv,
):
    ctx, me = lax.axis_index("ctx"), lax.axis_index("head")
    z, core = ctx // 2, lax.rem(ctx, 2)
    mx, my = me // YS, lax.rem(me, YS)
    other = z * 2 + 1 - core

    def peer(i, sign):
        o = lax.rem(i * 7, SHARDS)
        px = lax.rem(mx + XS + sign * (o // YS), XS)
        py = lax.rem(my + YS + sign * lax.rem(o, YS), YS)
        return px * YS + py

    def remote(src, dst, send, recv, c, h):
        return pltpu.make_async_remote_copy(
            src_ref=src, dst_ref=dst, send_sem=send, recv_sem=recv, device_id=(c, h), device_id_type=MESH
        )

    def log_copy(to, slot):
        return remote(log_own, log_all.at[slot], log_send.at[to], log_recv.at[slot], ctx, to)

    def s_copy(p, to, slot):
        return remote(s_out.at[p, to], s_in.at[p, slot], s_send.at[p, to], s_recv.at[p, slot], ctx, to)

    def p_copy(p, to, slot):
        return remote(p_out.at[p, to], p_in.at[p, slot], p_send.at[p, to], p_recv.at[p, slot], ctx, to)

    def shard_core_copy():
        return remote(shard_own.at[core], shard_own.at[core], shard_send.at[ZS], shard_recv.at[ZS], other, me)

    def shard_core_wait():
        return remote(shard_own.at[1 - core], shard_own.at[1 - core], shard_send.at[ZS], shard_recv.at[ZS], other, me)

    def shard_copy(to, slot):
        return remote(shard_own, shard_all.at[slot], shard_send.at[to], shard_recv.at[slot], to * 2 + core, me)

    def z_copy(p, to, slot):
        return remote(zsum_own.at[p], zsum_in.at[p, slot], z_send.at[p, to], z_recv.at[p, slot], to * 2 + core, me)

    def pair_copy(p):
        return remote(pair_out.at[p], pair_in.at[p], core_send.at[p], core_recv.at[p], other, me)

    def back_copy(p):
        return remote(back_out.at[p], back_in.at[p], back_send.at[p], back_recv.at[p], other, me)

    def x_load(g):
        cols = pl.ds(pl.multiple_of(g * GCOLS, GCOLS), GCOLS)
        return pltpu.make_async_copy(x_hbm.at[:, cols], xv.at[:, cols], load_sem.at[g])

    b_load = pltpu.make_async_copy(b_hbm, bv, b_sem.at[0])
    c_load = pltpu.make_async_copy(c_hbm, cv, b_sem.at[1])
    small = [
        pltpu.make_async_copy(src, dst, b_sem.at[2 + i])
        for i, (src, dst) in enumerate(
            ((dt_hbm, dt_ref), (rate_hbm, rate_ref), (bias_hbm, bias_ref), (skip_hbm, skip_ref))
        )
    ]
    for load in small:
        load.start()
    b_load.start()

    def start_load(i, carry):
        x_load(lax.rem(me // 2 + 1 + i, GROUPS)).start()
        return carry

    lax.fori_loop(0, GROUPS, start_load, 0)
    c_load.start()

    shard_all[...] = jnp.zeros_like(shard_all)
    barrier = pltpu.get_barrier_semaphore()

    def greet_head(i, carry):
        pl.semaphore_signal(barrier, inc=1, device_id=(ctx, peer(i, 1)), device_id_type=MESH)
        return carry

    lax.fori_loop(1, SHARDS, greet_head, 0)

    def greet_z(to, carry):
        pl.semaphore_signal(barrier, inc=1, device_id=(to * 2 + core, me), device_id_type=MESH)
        return carry

    lax.fori_loop(z + 1, ZS, greet_z, 0)
    pl.semaphore_signal(barrier, inc=1, device_id=(other, me), device_id_type=MESH)

    for load in small:
        load.wait()
    raw = dt_ref[...].astype(F32) + bias_ref[...]
    step = jnp.maximum(raw, 0.0) + jnp.log1p(jnp.exp(-jnp.abs(raw)))
    log_decay = -rate_ref[...] * step
    lower = iota((ROWS, ROWS), 0) >= iota((ROWS, ROWS), 1)
    within = dot(lower.astype(F32), log_decay, precision=HI)
    total = within[ROWS - 1 : ROWS, :]
    log_own[...] = jnp.broadcast_to(total, (8, HEADS))
    end_weight = two_parts(jnp.exp(total - within) * step)
    in_weight = two_parts(jnp.exp(within))
    skip_hl = two_parts(jnp.broadcast_to(skip_ref[...], (16, HEADS)))
    scaled = within * LOG2E
    scaled_t = jnp.transpose(scaled)
    step_t = jnp.transpose(step)
    for g in range(GROUPS):
        lo, hi = g * PER, (g + 1) * PER
        for ref, value in ((end_parts, end_weight), (in_parts, in_weight), (skip_parts, skip_hl)):
            ref[g] = jnp.concatenate([value[:, lo:hi], value[:, HEADS + lo : HEADS + hi]], axis=1)
        cum_cols[g] = scaled[:, lo:hi]
        cum_rows[g] = scaled_t[lo:hi, :]
        dt_rows[g] = step_t[lo:hi, :]
    spread[...] = (lax.rem(iota((2 * PER, GCOLS), 0), PER) == iota((2 * PER, GCOLS), 1) // WIDTH).astype(BF)

    order_row, order_col = iota((256, 256), 0), iota((256, 256), 1)
    order = (order_col == lax.rem(order_row, 32) * GROUPS + order_row // 32).astype(BF)

    def regroup(src, dst):
        for strip in range(ROWS // 32):
            part = dot(order, src[strip * 256 : (strip + 1) * 256, :]).astype(BF)
            for g in range(GROUPS):
                dst[g, strip * 32 : (strip + 1) * 32, :] = part[g * 32 : (g + 1) * 32, :]

    b_load.wait()
    regroup(bv, bg)

    pl.semaphore_wait(barrier, SHARDS - 1 + z + 1)

    def tell_back(back, carry):
        pl.semaphore_signal(ready, inc=1, device_id=(back * 2 + core, me), device_id_type=MESH)
        return carry

    lax.fori_loop(0, z, tell_back, 0)

    def send_logs(i, carry):
        log_copy(peer(i, 1), me).start()
        return carry

    lax.fori_loop(1, SHARDS, send_logs, 0)

    def own_state(i, carry):
        g = lax.rem(me // 2 + 1 + i, GROUPS)
        x_load(g).wait()
        cols = pl.ds(pl.multiple_of(g * GCOLS, GCOLS), GCOLS)
        weight = dot(end_parts[g], spread[...])
        xs = (xv[:, cols].astype(F32) * weight).astype(BF)
        value = dot(bg[g], xs, ((0,), (0,))).astype(BF)
        for a in range(2):
            for p in range(PIECES):
                at = a * OWN + p * COLS
                s_out[p, 2 * g + a] = value[:, at : at + COLS]
        for a in range(2):

            @pl.when(2 * g + a != me)
            def _():
                s_copy(0, 2 * g + a, me).start()

        return carry

    lax.fori_loop(0, GROUPS, own_state, 0)
    for p in range(1, PIECES):

        def send_s(i, carry):
            s_copy(p, peer(i, 1), me).start()
            return carry

        lax.fori_loop(1, SHARDS, send_s, 0)

    c_load.wait()
    regroup(cv, cg)

    lane = iota((ROWS, 2 * WIDTH), 1)

    def inside(g, carry):
        scores = jnp.where(lower, dot(cg[g], bg[g], ((1,), (1,))), 0.0)
        skip = dot(skip_parts[g], spread[...])
        col, row, dts = cum_cols[g], cum_rows[g], dt_rows[g]
        for pair in range(PER // 2):
            parts = []
            for h in (2 * pair, 2 * pair + 1):
                span = col[:, h : h + 1] - row[h : h + 1, :]
                decay = jnp.exp2(jnp.minimum(span, 0.0))
                parts.append((scores * decay * dts[h : h + 1, :]).astype(BF))
            at = pair * 2 * WIDTH
            x2 = xv[:, pl.ds(pl.multiple_of(g * GCOLS + at, 2 * WIDTH), 2 * WIDTH)]
            zero = jnp.zeros_like(x2)
            blocks = jnp.concatenate(
                [jnp.where(lane < WIDTH, x2, zero), jnp.where(lane < WIDTH, zero, x2)], axis=0
            )
            value = dot(jnp.concatenate(parts, axis=1), blocks)
            value = value + skip[0:1, at : at + 2 * WIDTH] * x2.astype(F32)
            acc[2 * g + at // OWN, :, at % OWN : at % OWN + 2 * WIDTH] = value
        weight = dot(in_parts[g], spread[...])
        ew[2 * g] = weight[:, :OWN]
        ew[2 * g + 1] = weight[:, OWN:]
        return carry

    lax.fori_loop(0, 2, inside, 0)

    def logs_in(i, carry):
        src = peer(i, -1)
        log_copy(src, src).wait_recv()
        return carry

    lax.fori_loop(1, SHARDS, logs_in, 0)
    log_all[me] = log_own[...]
    logs = log_all[:, 0, :]
    shard_log = jnp.sum(logs, axis=0, keepdims=True)
    shard_own[core] = jnp.broadcast_to(shard_log, (8, HEADS))
    shard_core_copy().start()
    later = (iota((SHARDS, SHARDS), 1) > iota((SHARDS, SHARDS), 0)).astype(F32)
    to_end = dot(later, logs, precision=HI)
    mine = (iota((HEADS, OWN), 0) == me * (HEADS // SHARDS) + iota((HEADS, OWN), 1) // WIDTH).astype(F32)
    chunk_decay = jnp.exp(dot(logs, mine, precision=HI))
    end_decay = jnp.exp(dot(to_end, mine, precision=HI))
    for j in range(SHARDS):
        end_rows[j] = jnp.broadcast_to(end_decay[j : j + 1, :], (8, OWN))

    lax.fori_loop(2, 4, inside, 0)
    shard_core_wait().wait_recv()

    pair_decay = jnp.exp(dot(shard_own[:, 0, :], mine, precision=HI))

    def exchange_logs():
        @pl.when(z < ZS - 1)
        def _():
            pl.semaphore_wait(ready, ZS - 1 - z)

        def send_shard(to, carry):
            shard_copy(to, z).start()
            return carry

        lax.fori_loop(z + 1, ZS, send_shard, 0)

    def z_tables():
        def shard_wait(src, carry):
            shard_copy(src, src).wait_recv()
            return carry

        lax.fori_loop(0, z, shard_wait, 0)
        pair_logs = shard_all[:, 0, 0, :] + shard_all[:, 1, 0, :]
        zi, zj = iota((ZS, ZS), 0), iota((ZS, ZS), 1)
        between = ((zj > zi) & (zj < z)).astype(F32)
        z_logs = dot(between, pair_logs, precision=HI)
        z_weight = jnp.exp(dot(z_logs, mine, precision=HI))
        for j in range(ZS):
            z_rows[j] = jnp.broadcast_to(z_weight[j : j + 1, :], (8, OWN))

    def half(value, which):
        return jnp.where(which == 0, value[:HALF, :], value[HALF:, :])

    def gather(p):
        cols = slice(p * COLS, (p + 1) * COLS)
        s_in[p, me] = s_out[p, me]
        total_state[...] = end_rows[me][0:1, cols] * s_in[p, me].astype(F32)

        def s_wait(i, carry):
            src = peer(i, -1)
            s_copy(p, src, src).wait_recv()
            total_state[...] += end_rows[src][0:1, cols] * s_in[p, src].astype(F32)
            return carry

        lax.fori_loop(1, SHARDS, s_wait, 0)
        value = total_state[...]
        keep = half(value, core)
        pair_out[p] = half(value, 1 - core).astype(BF)
        pair_copy(p).start()
        pair_copy(p).wait_recv()
        theirs = pair_in[p].astype(F32)
        first = jnp.where(core == 0, keep, theirs)
        second = jnp.where(core == 0, theirs, keep)
        zsum_own[p] = (first * pair_decay[1:2, cols] + second).astype(BF)

        def z_start(to, carry):
            z_copy(p, to, z).start()
            return carry

        lax.fori_loop(z + 1, ZS, z_start, 0)
        firsts[p] = first

    def give_back(p):
        cols = slice(p * COLS, (p + 1) * COLS)
        before_state[...] = jnp.zeros_like(before_state)

        def z_wait(src, carry):
            z_copy(p, src, src).wait_recv()
            before_state[...] += z_rows[src][0:1, cols] * zsum_in[p, src].astype(F32)
            return carry

        lax.fori_loop(0, z, z_wait, 0)
        before = before_state[...]
        after = before * pair_decay[0:1, cols] + firsts[p]
        back_out[p] = jnp.where(core == 0, after, before).astype(BF)
        back_copy(p).start()
        back_copy(p).wait_recv()
        keep = jnp.where(core == 0, before, after)
        theirs = back_in[p].astype(F32)
        state = jnp.where(
            core == 0, jnp.concatenate([keep, theirs], axis=0), jnp.concatenate([theirs, keep], axis=0)
        )
        for j in range(SHARDS):
            p_out[p, j] = state.astype(BF)
            if j < SHARDS - 1:
                state = state * chunk_decay[j : j + 1, cols] + s_in[p, j].astype(F32)
        p_in[p, me] = p_out[p, me]

        def p_start(i, carry):
            p_copy(p, peer(i, 1), me).start()
            return carry

        lax.fori_loop(1, SHARDS, p_start, 0)

    def finish(p, k):
        across = dot(cg[k // 2], p_in[p, k])
        cols = slice(p * COLS, (p + 1) * COLS)
        value = (acc[k, :, cols] + ew[k, :, cols] * across).astype(BF)
        y_ref[:, pl.ds(pl.multiple_of(k * OWN + p * COLS, COLS), COLS)] = value

    exchange_logs()
    gather(0)
    lax.fori_loop(4, 6, inside, 0)
    gather(1)
    z_tables()
    give_back(0)
    lax.fori_loop(6, 7, inside, 0)
    gather(2)
    give_back(1)
    lax.fori_loop(7, GROUPS, inside, 0)
    gather(3)
    give_back(2)
    give_back(3)
    for p in range(PIECES):
        finish(p, me)

        def p_wait(i, carry):
            batch = [peer(3 * i + 1 + j, -1) for j in range(3)]
            for src in batch:
                p_copy(p, src, src).wait_recv()
            for src in batch:
                finish(p, src)
            return carry

        lax.fori_loop(0, (SHARDS - 1) // 3, p_wait, 0)

    def sent_head(i, carry):
        to = peer(i, 1)
        log_copy(to, me).wait_send()
        for p in range(PIECES):
            s_copy(p, to, me).wait_send()
            p_copy(p, to, me).wait_send()
        return carry

    lax.fori_loop(1, SHARDS, sent_head, 0)

    def sent_z(to, carry):
        shard_copy(to, z).wait_send()
        for p in range(PIECES):
            z_copy(p, to, z).wait_send()
        return carry

    lax.fori_loop(z + 1, ZS, sent_z, 0)
    shard_core_copy().wait_send()
    for p in range(PIECES):
        pair_copy(p).wait_send()
        back_copy(p).wait_send()


def per_device(x_in, b_in, c_in, dt_raw, decay_rate, dt_bias, skip_gain):
    vmem, dma = pltpu.VMEM, pltpu.SemaphoreType.DMA
    any_spec = pl.BlockSpec(memory_space=pltpu.HBM)
    return pl.pallas_call(
        kernel,
        name="scan",
        out_shape=pltpu.VMEM((ROWS, HEADS * WIDTH), BF),
        in_specs=[any_spec] * 7,
        out_specs=pl.BlockSpec(memory_space=pltpu.VMEM),
        scratch_shapes=[
            vmem((ROWS, HEADS), BF),
            vmem((1, HEADS), F32),
            vmem((1, HEADS), F32),
            vmem((1, HEADS), F32),
            vmem((ROWS, HEADS * WIDTH), BF),
            vmem((ROWS * GROUPS, STATE), BF),
            vmem((ROWS * GROUPS, STATE), BF),
            vmem((GROUPS, ROWS, STATE), BF),
            vmem((GROUPS, ROWS, STATE), BF),
            vmem((2 * PER, GCOLS), BF),
            vmem((GROUPS, ROWS, 2 * PER), BF),
            vmem((GROUPS, ROWS, 2 * PER), BF),
            vmem((GROUPS, 16, 2 * PER), BF),
            vmem((GROUPS, ROWS, PER), F32),
            vmem((GROUPS, PER, ROWS), F32),
            vmem((GROUPS, PER, ROWS), F32),
            vmem((PIECES, SHARDS, STATE, COLS), BF),
            vmem((PIECES, SHARDS, STATE, COLS), BF),
            vmem((PIECES, SHARDS, STATE, COLS), BF),
            vmem((PIECES, SHARDS, STATE, COLS), BF),
            vmem((SHARDS, ROWS, OWN), F32),
            vmem((SHARDS, ROWS, OWN), F32),
            vmem((8, HEADS), F32),
            vmem((SHARDS, 8, HEADS), F32),
            vmem((2, 8, HEADS), F32),
            vmem((ZS, 2, 8, HEADS), F32),
            vmem((PIECES, HALF, COLS), BF),
            vmem((PIECES, HALF, COLS), BF),
            vmem((PIECES, HALF, COLS), BF),
            vmem((PIECES, ZS, HALF, COLS), BF),
            vmem((PIECES, HALF, COLS), BF),
            vmem((PIECES, HALF, COLS), BF),
            vmem((SHARDS, 8, OWN), F32),
            vmem((ZS, 8, OWN), F32),
            vmem((STATE, COLS), F32),
            vmem((HALF, COLS), F32),
            vmem((PIECES, HALF, COLS), F32),
            pltpu.SemaphoreType.REGULAR,
            dma((GROUPS,)),
            dma((6,)),
            dma((PIECES, SHARDS)),
            dma((PIECES, SHARDS)),
            dma((PIECES, SHARDS)),
            dma((PIECES, SHARDS)),
            dma((SHARDS,)),
            dma((SHARDS,)),
            dma((ZS + 1,)),
            dma((ZS + 1,)),
            dma((PIECES,)),
            dma((PIECES,)),
            dma((PIECES, ZS)),
            dma((PIECES, ZS)),
            dma((PIECES,)),
            dma((PIECES,)),
        ],
        compiler_params=pltpu.CompilerParams(
            collective_id=0, has_side_effects=True, vmem_limit_bytes=61 * 1024 * 1024
        ),
    )(
        x_in,
        b_in.reshape(ROWS * GROUPS, STATE),
        c_in.reshape(ROWS * GROUPS, STATE),
        dt_raw,
        decay_rate.reshape(1, HEADS),
        dt_bias.reshape(1, HEADS),
        skip_gain.reshape(1, HEADS),
    )


def solution(mesh):
    rows = ("ctx", "head")
    in_specs = (P(rows, None), P(rows, None, None), P(rows, None, None), P(rows, None), P(), P(), P())
    return jax.shard_map(
        per_device, mesh=mesh, in_specs=in_specs, out_specs=P(rows, None), check_vma=False
    )
```

```python
import functools

import jax
import jax.numpy as jnp
from jax import lax
from jax.experimental import pallas as pl
from jax.experimental.pallas import tpu as pltpu
from jax.sharding import PartitionSpec as P

MESH = pl.DeviceIdType.MESH
BF, F32 = jnp.bfloat16, jnp.float32
LOG2E = 1.4426950408889634
ROWS = 128
HEADS, GROUPS, STATE, WIDTH = 128, 8, 128, 64
PER = HEADS // GROUPS
GCOLS = PER * WIDTH
SHARDS = 16
OWN = HEADS // SHARDS * WIDTH
PIECES = 4
COLS = OWN // PIECES
HALF = STATE // 2
XS, YS, ZS = 4, 4, 8
HI = lax.Precision.HIGHEST


def dot(a, b, dims=((1,), (0,)), precision=None):
    return lax.dot_general(a, b, (dims, ((), ())), precision=precision, preferred_element_type=F32)


def two_parts(a):
    hi = a.astype(BF)
    lo = (a - hi.astype(F32)).astype(BF)
    return jnp.concatenate([hi, lo], axis=1)


def iota(shape, dim):
    return lax.broadcasted_iota(jnp.int32, shape, dim)


def kernel(
    x_hbm, b_hbm, c_hbm, dt_hbm, rate_hbm, bias_hbm, skip_hbm, y_ref,
    dt_ref, rate_ref, bias_ref, skip_ref, xv, bv, cv, bg, cg, spread, end_parts, in_parts, skip_parts, cum_cols, cum_rows, dt_rows,
    s_out, s_in, p_out, p_in, acc, ew,
    log_own, log_all, shard_own, shard_all, pair_out, pair_in, zsum_own, zsum_in, back_out, back_in,
    end_rows, z_rows, total_state, before_state, firsts, ready,
    load_sem, b_sem, s_send, s_recv, p_send, p_recv, log_send, log_recv,
    shard_send, shard_recv, core_send, core_recv, z_send, z_recv, back_send, back_recv,
):
    ctx, me = lax.axis_index("ctx"), lax.axis_index("head")
    z, core = ctx // 2, lax.rem(ctx, 2)
    mx, my = me // YS, lax.rem(me, YS)
    other = z * 2 + 1 - core

    def peer(i, sign):
        o = lax.rem(i * 7, SHARDS)
        px = lax.rem(mx + XS + sign * (o // YS), XS)
        py = lax.rem(my + YS + sign * lax.rem(o, YS), YS)
        return px * YS + py

    def remote(src, dst, send, recv, c, h):
        return pltpu.make_async_remote_copy(
            src_ref=src, dst_ref=dst, send_sem=send, recv_sem=recv, device_id=(c, h), device_id_type=MESH
        )

    def log_copy(to, slot):
        return remote(log_own, log_all.at[slot], log_send.at[to], log_recv.at[slot], ctx, to)

    def s_copy(p, to, slot):
        return remote(s_out.at[p, to], s_in.at[p, slot], s_send.at[p, to], s_recv.at[p, slot], ctx, to)

    def p_copy(p, to, slot):
        return remote(p_out.at[p, to], p_in.at[p, slot], p_send.at[p, to], p_recv.at[p, slot], ctx, to)

    def shard_core_copy():
        return remote(shard_own.at[core], shard_own.at[core], shard_send.at[ZS], shard_recv.at[ZS], other, me)

    def shard_core_wait():
        return remote(shard_own.at[1 - core], shard_own.at[1 - core], shard_send.at[ZS], shard_recv.at[ZS], other, me)

    def shard_copy(to, slot):
        return remote(shard_own, shard_all.at[slot], shard_send.at[to], shard_recv.at[slot], to * 2 + core, me)

    def z_copy(p, to, slot):
        return remote(zsum_own.at[p], zsum_in.at[p, slot], z_send.at[p, to], z_recv.at[p, slot], to * 2 + core, me)

    def pair_copy(p):
        return remote(pair_out.at[p], pair_in.at[p], core_send.at[p], core_recv.at[p], other, me)

    def back_copy(p):
        return remote(back_out.at[p], back_in.at[p], back_send.at[p], back_recv.at[p], other, me)

    def x_load(g):
        cols = pl.ds(pl.multiple_of(g * GCOLS, GCOLS), GCOLS)
        return pltpu.make_async_copy(x_hbm.at[:, cols], xv.at[:, cols], load_sem.at[g])

    b_load = pltpu.make_async_copy(b_hbm, bv, b_sem.at[0])
    c_load = pltpu.make_async_copy(c_hbm, cv, b_sem.at[1])
    small = [
        pltpu.make_async_copy(src, dst, b_sem.at[2 + i])
        for i, (src, dst) in enumerate(
            ((dt_hbm, dt_ref), (rate_hbm, rate_ref), (bias_hbm, bias_ref), (skip_hbm, skip_ref))
        )
    ]
    for load in small:
        load.start()
    b_load.start()

    def start_load(i, carry):
        x_load(lax.rem(me // 2 + 1 + i, GROUPS)).start()
        return carry

    lax.fori_loop(0, GROUPS, start_load, 0)
    c_load.start()

    shard_all[...] = jnp.zeros_like(shard_all)
    barrier = pltpu.get_barrier_semaphore()

    def greet_head(i, carry):
        pl.semaphore_signal(barrier, inc=1, device_id=(ctx, peer(i, 1)), device_id_type=MESH)
        return carry

    lax.fori_loop(1, SHARDS, greet_head, 0)

    def greet_z(to, carry):
        pl.semaphore_signal(barrier, inc=1, device_id=(to * 2 + core, me), device_id_type=MESH)
        return carry

    lax.fori_loop(z + 1, ZS, greet_z, 0)
    pl.semaphore_signal(barrier, inc=1, device_id=(other, me), device_id_type=MESH)

    for load in small:
        load.wait()
    raw = dt_ref[...].astype(F32) + bias_ref[...]
    step = jnp.maximum(raw, 0.0) + jnp.log1p(jnp.exp(-jnp.abs(raw)))
    log_decay = -rate_ref[...] * step
    lower = iota((ROWS, ROWS), 0) >= iota((ROWS, ROWS), 1)
    within = dot(lower.astype(F32), log_decay, precision=HI)
    total = within[ROWS - 1 : ROWS, :]
    log_own[...] = jnp.broadcast_to(total, (8, HEADS))
    end_weight = two_parts(jnp.exp(total - within) * step)
    in_weight = two_parts(jnp.exp(within))
    skip_hl = two_parts(jnp.broadcast_to(skip_ref[...], (16, HEADS)))
    scaled = within * LOG2E
    scaled_t = jnp.transpose(scaled)
    step_t = jnp.transpose(step)
    for g in range(GROUPS):
        lo, hi = g * PER, (g + 1) * PER
        for ref, value in ((end_parts, end_weight), (in_parts, in_weight), (skip_parts, skip_hl)):
            ref[g] = jnp.concatenate([value[:, lo:hi], value[:, HEADS + lo : HEADS + hi]], axis=1)
        cum_cols[g] = scaled[:, lo:hi]
        cum_rows[g] = scaled_t[lo:hi, :]
        dt_rows[g] = step_t[lo:hi, :]
    spread[...] = (lax.rem(iota((2 * PER, GCOLS), 0), PER) == iota((2 * PER, GCOLS), 1) // WIDTH).astype(BF)

    order_row, order_col = iota((256, 256), 0), iota((256, 256), 1)
    order = (order_col == lax.rem(order_row, 32) * GROUPS + order_row // 32).astype(BF)

    def regroup(src, dst):
        for strip in range(ROWS // 32):
            part = dot(order, src[strip * 256 : (strip + 1) * 256, :]).astype(BF)
            for g in range(GROUPS):
                dst[g, strip * 32 : (strip + 1) * 32, :] = part[g * 32 : (g + 1) * 32, :]

    b_load.wait()
    regroup(bv, bg)

    pl.semaphore_wait(barrier, SHARDS - 1 + z + 1)

    def tell_back(back, carry):
        pl.semaphore_signal(ready, inc=1, device_id=(back * 2 + core, me), device_id_type=MESH)
        return carry

    lax.fori_loop(0, z, tell_back, 0)

    def send_logs(i, carry):
        log_copy(peer(i, 1), me).start()
        return carry

    lax.fori_loop(1, SHARDS, send_logs, 0)

    def own_state(i, carry):
        g = lax.rem(me // 2 + 1 + i, GROUPS)
        x_load(g).wait()
        cols = pl.ds(pl.multiple_of(g * GCOLS, GCOLS), GCOLS)
        weight = dot(end_parts[g], spread[...])
        xs = (xv[:, cols].astype(F32) * weight).astype(BF)
        value = dot(bg[g], xs, ((0,), (0,))).astype(BF)
        for a in range(2):
            for p in range(PIECES):
                at = a * OWN + p * COLS
                s_out[p, 2 * g + a] = value[:, at : at + COLS]
        for a in range(2):

            @pl.when(2 * g + a != me)
            def _():
                s_copy(0, 2 * g + a, me).start()

        return carry

    lax.fori_loop(0, GROUPS, own_state, 0)
    for p in range(1, PIECES):

        def send_s(i, carry):
            s_copy(p, peer(i, 1), me).start()
            return carry

        lax.fori_loop(1, SHARDS, send_s, 0)

    c_load.wait()
    regroup(cv, cg)

    lane = iota((ROWS, 2 * WIDTH), 1)

    def inside(g, carry):
        scores = jnp.where(lower, dot(cg[g], bg[g], ((1,), (1,))), 0.0)
        skip = dot(skip_parts[g], spread[...])
        col, row, dts = cum_cols[g], cum_rows[g], dt_rows[g]
        for pair in range(PER // 2):
            parts = []
            for h in (2 * pair, 2 * pair + 1):
                span = col[:, h : h + 1] - row[h : h + 1, :]
                decay = jnp.exp2(jnp.minimum(span, 0.0))
                parts.append((scores * decay * dts[h : h + 1, :]).astype(BF))
            at = pair * 2 * WIDTH
            x2 = xv[:, pl.ds(pl.multiple_of(g * GCOLS + at, 2 * WIDTH), 2 * WIDTH)]
            zero = jnp.zeros_like(x2)
            blocks = jnp.concatenate(
                [jnp.where(lane < WIDTH, x2, zero), jnp.where(lane < WIDTH, zero, x2)], axis=0
            )
            value = dot(jnp.concatenate(parts, axis=1), blocks)
            value = value + skip[0:1, at : at + 2 * WIDTH] * x2.astype(F32)
            acc[2 * g + at // OWN, :, at % OWN : at % OWN + 2 * WIDTH] = value
        weight = dot(in_parts[g], spread[...])
        ew[2 * g] = weight[:, :OWN]
        ew[2 * g + 1] = weight[:, OWN:]
        return carry

    lax.fori_loop(0, 2, inside, 0)

    def logs_in(i, carry):
        src = peer(i, -1)
        log_copy(src, src).wait_recv()
        return carry

    lax.fori_loop(1, SHARDS, logs_in, 0)
    log_all[me] = log_own[...]
    logs = log_all[:, 0, :]
    shard_log = jnp.sum(logs, axis=0, keepdims=True)
    shard_own[core] = jnp.broadcast_to(shard_log, (8, HEADS))
    shard_core_copy().start()
    later = (iota((SHARDS, SHARDS), 1) > iota((SHARDS, SHARDS), 0)).astype(F32)
    to_end = dot(later, logs, precision=HI)
    mine = (iota((HEADS, OWN), 0) == me * (HEADS // SHARDS) + iota((HEADS, OWN), 1) // WIDTH).astype(F32)
    chunk_decay = jnp.exp(dot(logs, mine, precision=HI))
    end_decay = jnp.exp(dot(to_end, mine, precision=HI))
    for j in range(SHARDS):
        end_rows[j] = jnp.broadcast_to(end_decay[j : j + 1, :], (8, OWN))

    lax.fori_loop(2, 4, inside, 0)
    shard_core_wait().wait_recv()

    pair_decay = jnp.exp(dot(shard_own[:, 0, :], mine, precision=HI))

    def exchange_logs():
        @pl.when(z < ZS - 1)
        def _():
            pl.semaphore_wait(ready, ZS - 1 - z)

        def send_shard(to, carry):
            shard_copy(to, z).start()
            return carry

        lax.fori_loop(z + 1, ZS, send_shard, 0)

    def z_tables():
        def shard_wait(src, carry):
            shard_copy(src, src).wait_recv()
            return carry

        lax.fori_loop(0, z, shard_wait, 0)
        pair_logs = shard_all[:, 0, 0, :] + shard_all[:, 1, 0, :]
        zi, zj = iota((ZS, ZS), 0), iota((ZS, ZS), 1)
        between = ((zj > zi) & (zj < z)).astype(F32)
        z_logs = dot(between, pair_logs, precision=HI)
        z_weight = jnp.exp(dot(z_logs, mine, precision=HI))
        for j in range(ZS):
            z_rows[j] = jnp.broadcast_to(z_weight[j : j + 1, :], (8, OWN))

    def half(value, which):
        return jnp.where(which == 0, value[:HALF, :], value[HALF:, :])

    def gather(p):
        cols = slice(p * COLS, (p + 1) * COLS)
        s_in[p, me] = s_out[p, me]
        total_state[...] = end_rows[me][0:1, cols] * s_in[p, me].astype(F32)

        def s_wait(i, carry):
            src = peer(i, -1)
            s_copy(p, src, src).wait_recv()
            total_state[...] += end_rows[src][0:1, cols] * s_in[p, src].astype(F32)
            return carry

        lax.fori_loop(1, SHARDS, s_wait, 0)
        value = total_state[...]
        keep = half(value, core)
        pair_out[p] = half(value, 1 - core).astype(BF)
        pair_copy(p).start()
        pair_copy(p).wait_recv()
        theirs = pair_in[p].astype(F32)
        first = jnp.where(core == 0, keep, theirs)
        second = jnp.where(core == 0, theirs, keep)
        zsum_own[p] = (first * pair_decay[1:2, cols] + second).astype(BF)

        def z_start(to, carry):
            z_copy(p, to, z).start()
            return carry

        lax.fori_loop(z + 1, ZS, z_start, 0)
        firsts[p] = first

    def give_back(p):
        cols = slice(p * COLS, (p + 1) * COLS)
        before_state[...] = jnp.zeros_like(before_state)

        def z_wait(src, carry):
            z_copy(p, src, src).wait_recv()
            before_state[...] += z_rows[src][0:1, cols] * zsum_in[p, src].astype(F32)
            return carry

        lax.fori_loop(0, z, z_wait, 0)
        before = before_state[...]
        after = before * pair_decay[0:1, cols] + firsts[p]
        back_out[p] = jnp.where(core == 0, after, before).astype(BF)
        back_copy(p).start()
        back_copy(p).wait_recv()
        keep = jnp.where(core == 0, before, after)
        theirs = back_in[p].astype(F32)
        state = jnp.where(
            core == 0, jnp.concatenate([keep, theirs], axis=0), jnp.concatenate([theirs, keep], axis=0)
        )
        for j in range(SHARDS):
            p_out[p, j] = state.astype(BF)
            if j < SHARDS - 1:
                state = state * chunk_decay[j : j + 1, cols] + s_in[p, j].astype(F32)
        p_in[p, me] = p_out[p, me]

        def p_start(i, carry):
            p_copy(p, peer(i, 1), me).start()
            return carry

        lax.fori_loop(1, SHARDS, p_start, 0)

    def finish(p, k):
        across = dot(cg[k // 2], p_in[p, k])
        cols = slice(p * COLS, (p + 1) * COLS)
        value = (acc[k, :, cols] + ew[k, :, cols] * across).astype(BF)
        y_ref[:, pl.ds(pl.multiple_of(k * OWN + p * COLS, COLS), COLS)] = value

    exchange_logs()
    gather(0)
    lax.fori_loop(4, 6, inside, 0)
    gather(1)
    z_tables()
    give_back(0)
    lax.fori_loop(6, 7, inside, 0)
    gather(2)
    give_back(1)
    lax.fori_loop(7, GROUPS, inside, 0)
    gather(3)
    give_back(2)
    give_back(3)
    def sent_head(i, carry):
        to = peer(i, 1)
        log_copy(to, me).wait_send()
        for p in range(PIECES):
            s_copy(p, to, me).wait_send()
        return carry

    lax.fori_loop(1, SHARDS, sent_head, 0)

    def sent_z(to, carry):
        shard_copy(to, z).wait_send()
        for p in range(PIECES):
            z_copy(p, to, z).wait_send()
        return carry

    lax.fori_loop(z + 1, ZS, sent_z, 0)
    shard_core_copy().wait_send()
    for p in range(PIECES):
        pair_copy(p).wait_send()
        back_copy(p).wait_send()

    for p in range(PIECES):
        if p == PIECES - 1:
            for q in range(PIECES):

                def sent_p(i, carry):
                    p_copy(q, peer(i, 1), me).wait_send()
                    return carry

                lax.fori_loop(1, SHARDS, sent_p, 0)
        finish(p, me)

        def p_wait(i, carry):
            batch = [peer(5 * i + 1 + j, -1) for j in range(5)]
            for src in batch:
                p_copy(p, src, src).wait_recv()
            for src in batch:
                finish(p, src)
            return carry

        lax.fori_loop(0, (SHARDS - 1) // 5, p_wait, 0)


def per_device(x_in, b_in, c_in, dt_raw, decay_rate, dt_bias, skip_gain):
    vmem, dma = pltpu.VMEM, pltpu.SemaphoreType.DMA
    any_spec = pl.BlockSpec(memory_space=pltpu.HBM)
    return pl.pallas_call(
        kernel,
        name="scan",
        out_shape=pltpu.VMEM((ROWS, HEADS * WIDTH), BF),
        in_specs=[any_spec] * 7,
        out_specs=pl.BlockSpec(memory_space=pltpu.VMEM),
        scratch_shapes=[
            vmem((ROWS, HEADS), BF),
            vmem((1, HEADS), F32),
            vmem((1, HEADS), F32),
            vmem((1, HEADS), F32),
            vmem((ROWS, HEADS * WIDTH), BF),
            vmem((ROWS * GROUPS, STATE), BF),
            vmem((ROWS * GROUPS, STATE), BF),
            vmem((GROUPS, ROWS, STATE), BF),
            vmem((GROUPS, ROWS, STATE), BF),
            vmem((2 * PER, GCOLS), BF),
            vmem((GROUPS, ROWS, 2 * PER), BF),
            vmem((GROUPS, ROWS, 2 * PER), BF),
            vmem((GROUPS, 16, 2 * PER), BF),
            vmem((GROUPS, ROWS, PER), F32),
            vmem((GROUPS, PER, ROWS), F32),
            vmem((GROUPS, PER, ROWS), F32),
            vmem((PIECES, SHARDS, STATE, COLS), BF),
            vmem((PIECES, SHARDS, STATE, COLS), BF),
            vmem((PIECES, SHARDS, STATE, COLS), BF),
            vmem((PIECES, SHARDS, STATE, COLS), BF),
            vmem((SHARDS, ROWS, OWN), F32),
            vmem((SHARDS, ROWS, OWN), F32),
            vmem((8, HEADS), F32),
            vmem((SHARDS, 8, HEADS), F32),
            vmem((2, 8, HEADS), F32),
            vmem((ZS, 2, 8, HEADS), F32),
            vmem((PIECES, HALF, COLS), BF),
            vmem((PIECES, HALF, COLS), BF),
            vmem((PIECES, HALF, COLS), BF),
            vmem((PIECES, ZS, HALF, COLS), BF),
            vmem((PIECES, HALF, COLS), BF),
            vmem((PIECES, HALF, COLS), BF),
            vmem((SHARDS, 8, OWN), F32),
            vmem((ZS, 8, OWN), F32),
            vmem((STATE, COLS), F32),
            vmem((HALF, COLS), F32),
            vmem((PIECES, HALF, COLS), F32),
            pltpu.SemaphoreType.REGULAR,
            dma((GROUPS,)),
            dma((6,)),
            dma((PIECES, SHARDS)),
            dma((PIECES, SHARDS)),
            dma((PIECES, SHARDS)),
            dma((PIECES, SHARDS)),
            dma((SHARDS,)),
            dma((SHARDS,)),
            dma((ZS + 1,)),
            dma((ZS + 1,)),
            dma((PIECES,)),
            dma((PIECES,)),
            dma((PIECES, ZS)),
            dma((PIECES, ZS)),
            dma((PIECES,)),
            dma((PIECES,)),
        ],
        compiler_params=pltpu.CompilerParams(
            collective_id=0, has_side_effects=True, vmem_limit_bytes=61 * 1024 * 1024
        ),
    )(
        x_in,
        b_in.reshape(ROWS * GROUPS, STATE),
        c_in.reshape(ROWS * GROUPS, STATE),
        dt_raw,
        decay_rate.reshape(1, HEADS),
        dt_bias.reshape(1, HEADS),
        skip_gain.reshape(1, HEADS),
    )


def solution(mesh):
    rows = ("ctx", "head")
    in_specs = (P(rows, None), P(rows, None, None), P(rows, None, None), P(rows, None), P(), P(), P())
    return jax.shard_map(
        per_device, mesh=mesh, in_specs=in_specs, out_specs=P(rows, None), check_vma=False
    )
```
